256 devices in a mesh: vec: 32 (over y, z), field: 4 (over x_lo, core), rep: 2 (over x_hi).
Axes of the slice: x: 4 (x_hi: 2, x_lo: 2; x = x_hi * 2 + x_lo), y: 4, z: 8, core: 2. Of those that a mesh axis runs over, the one named last changes fastest.
Arguments:
- dosage: bfloat16 [768, 65536], P('vec', 'field'), may hold values from 0 to 2
Outputs:
- ccc: float32 [2, 768, 2, 24, 2, 96], P('rep', ('vec', 'field'))
The draws below stay inside these ranges and needn't reach their ends.
All inputs are finite; a program needn't handle non-finite values.
Results may differ from the reference program's by a relative error of at most 0.0003.
Values may be sent and summed in bfloat16 or wider, within the bound.
No kernel may reach another device: no remote copies, remote signals or barrier semaphores. Data moves between devices by JAX's collectives and lax.ppermute only.
A program may use at most 64 MiB of HBM per device.

```python
import jax
import jax.numpy as jnp
from jax import lax

F = 65536
VB = 24
S = 2
V = 768
N_VEC = 32
N_REP = 2


def draw_dosage(key, part):
    freq_key, noise_key = jax.random.split(jax.random.fold_in(key, 11), 2)
    position = jnp.arange(F, dtype=jnp.float32) / F
    allele = (0.12 + 0.6 * position) * jax.random.uniform(freq_key, (F,), jnp.float32, 0.6, 1.4)
    dosage_value = 2.0 * allele[None, :] + 0.5 * jax.random.normal(noise_key, (V, F), jnp.float32)
    return jnp.clip(dosage_value, 0.0, 2.0).astype(jnp.bfloat16)


def setup_inputs(seed: int = 0) -> dict:
    key_list = jax.random.split(jax.random.key(seed), 2)
    dosage = draw_dosage(jax.random.fold_in(key_list[1], 71), 0)
    return {"dosage": dosage}


def contract_rows(first_rows, third_rows, partner_rows):
    field_width = first_rows.shape[1]
    block_width = min(2048, field_width)
    block_count = field_width // block_width

    def add_block(running, block_id):
        offset = block_id * block_width
        first_cut = lax.dynamic_slice_in_dim(first_rows, offset, block_width, 1)
        third_cut = lax.dynamic_slice_in_dim(third_rows, offset, block_width, 1)
        partner_cut = lax.dynamic_slice_in_dim(partner_rows, offset, block_width, 1)
        pair_rows = (first_cut[:, None, :] * third_cut[None, :, :]).reshape(-1, block_width)
        running = running + lax.dot_general(pair_rows.astype(jnp.float32), partner_cut.astype(jnp.float32), (((1,), (1,)), ((), ())), precision=lax.Precision.HIGHEST, preferred_element_type=jnp.float32)
        return running, None

    start_value = jnp.zeros((first_rows.shape[0] * third_rows.shape[0], partner_rows.shape[0]), jnp.float32)
    running, unused = lax.scan(add_block, start_value, jnp.arange(block_count, dtype=jnp.int32))
    return running


def reference(dosage):
    other_count = (2.0 - dosage.astype(jnp.float32)).astype(jnp.bfloat16)
    stacked = jnp.stack([other_count, dosage], axis=1)
    totals = jnp.sum(stacked.astype(jnp.float32), axis=2)
    gain_all = (1.0 - totals / (3.0 * F)).reshape(N_VEC, VB, 2)
    vector_rows = stacked.reshape(N_VEC, 2 * VB, F)
    planes = []
    for rep_plane in range(N_REP):
        def plane_block(block_id):
            third_id = (block_id - 1 - rep_plane) % N_VEC
            partner_ids = (block_id + 1 + jnp.arange(S, dtype=jnp.int32)) % N_VEC
            partner_rows = vector_rows[partner_ids].reshape(S * 2 * VB, F)
            tables = contract_rows(vector_rows[block_id], vector_rows[third_id], partner_rows)
            tables = tables.reshape(VB, 2, VB, 2, S * 2 * VB)
            gain_first = gain_all[block_id]
            gain_third = gain_all[third_id]
            gain_partner = gain_all[partner_ids].reshape(-1)
            return (4.5 / (8.0 * F)) * tables * gain_first[:, :, None, None, None] * gain_third[None, None, :, :, None] * gain_partner
        planes.append(lax.map(plane_block, jnp.arange(N_VEC, dtype=jnp.int32)))
    return jnp.stack(planes).reshape(N_REP, V, 2, VB, 2, S * 2 * VB)
```

```python
import jax
import jax.numpy as jnp
from jax import lax
from jax.experimental import pallas as pl
from jax.experimental.pallas import tpu as pltpu
from jax.sharding import PartitionSpec as P

F = 65536
VB = 24
N_VEC = 32
N_FIELD = 4
N_REP = 2
SHARE = VB // N_FIELD
CHUNKS = 2
STEP = 1024
PAIRS = VB * 2 * VB
ROWS = PAIRS + 96
COLS = 64
PACKED = 96


def shifted(value, by):
    return lax.ppermute(value, "vec", [(i, (i + by) % N_VEC) for i in range(N_VEC)])


def fill_and_multiply(u_ref, a1_ref, a2_ref, b1_ref, b2_ref, lhs_ref):
    width = u_ref.shape[1]
    own = u_ref[...]
    third = jnp.concatenate([a1_ref[...], a2_ref[...]], axis=0)
    for i in range(VB):
        lhs_ref[i * 48 : (i + 1) * 48, :] = own[i : i + 1, :] * third
    ones = jnp.ones((VB, width), jnp.bfloat16)
    lhs_ref[PAIRS:, :] = jnp.concatenate([third, own, ones], axis=0)
    partner = jnp.concatenate([b1_ref[...], b2_ref[...], ones[:16]], axis=0)
    return lax.dot_general(
        lhs_ref[...], partner, (((1,), (1,)), ((), ())), preferred_element_type=jnp.float32
    )


def pack(acc_ref, out_ref):
    for q in range(N_FIELD):
        singles = jnp.concatenate(
            [
                acc_ref[PAIRS + 72 : PAIRS + 73, :],
                acc_ref[PAIRS + 48 + SHARE * q : PAIRS + 48 + SHARE * (q + 1), :],
                jnp.zeros((1, COLS), jnp.float32),
            ],
            axis=0,
        )
        for r in range(N_REP):
            dest = r * N_FIELD + q
            for ii in range(3):
                for half in range(2):
                    row = (SHARE * q + 3 * half + ii) * 48 + VB * r
                    out_ref[dest, ii * VB : (ii + 1) * VB, half * COLS : (half + 1) * COLS] = acc_ref[
                        row : row + VB, :
                    ]
            out_ref[dest, 72:96, :COLS] = acc_ref[PAIRS + VB * r : PAIRS + VB * (r + 1), :]
            out_ref[dest, 72:80, COLS:] = singles
            out_ref[dest, 80:96, COLS:] = jnp.zeros((16, COLS), jnp.float32)


def first_kernel(u_ref, a1_ref, a2_ref, b1_ref, b2_ref, acc_ref, lhs_ref):
    product = fill_and_multiply(u_ref, a1_ref, a2_ref, b1_ref, b2_ref, lhs_ref)

    @pl.when(pl.program_id(0) == 0)
    def _():
        acc_ref[...] = product

    @pl.when(pl.program_id(0) > 0)
    def _():
        acc_ref[...] += product


def last_kernel(u_ref, a1_ref, a2_ref, b1_ref, b2_ref, before_ref, out_ref, lhs_ref, acc_ref):
    product = fill_and_multiply(u_ref, a1_ref, a2_ref, b1_ref, b2_ref, lhs_ref)

    @pl.when(pl.program_id(0) == 0)
    def _():
        acc_ref[...] = before_ref[...] + product

    @pl.when(pl.program_id(0) > 0)
    def _():
        acc_ref[...] += product

    @pl.when(pl.program_id(0) == pl.num_programs(0) - 1)
    def _():
        pack(acc_ref, out_ref)


def tables_of(blocks, before):
    width = blocks[0].shape[1]
    steps = width // STEP
    block_spec = pl.BlockSpec((VB, STEP), lambda s: (0, s))
    acc_spec = pl.BlockSpec((ROWS, COLS), lambda s: (0, 0))
    cost = pl.CostEstimate(
        flops=2 * ROWS * width * 256, bytes_accessed=5 * VB * width * 2, transcendentals=0
    )
    params = pltpu.CompilerParams(vmem_limit_bytes=32 * 2**20)
    lhs = pltpu.VMEM((ROWS, STEP), jnp.bfloat16)
    if before is None:
        return pl.pallas_call(
            first_kernel,
            grid=(steps,),
            in_specs=[block_spec] * 5,
            out_specs=acc_spec,
            out_shape=jax.ShapeDtypeStruct((ROWS, COLS), jnp.float32),
            scratch_shapes=[lhs],
            compiler_params=params,
            cost_estimate=cost,
            name="tables_first",
        )(*blocks)
    return pl.pallas_call(
        last_kernel,
        grid=(steps,),
        in_specs=[block_spec] * 5 + [acc_spec],
        out_specs=pl.BlockSpec((8, PACKED, 128), lambda s: (0, 0, 0)),
        out_shape=jax.ShapeDtypeStruct((8, PACKED, 128), jnp.float32),
        scratch_shapes=[lhs, pltpu.VMEM((ROWS, COLS), jnp.float32)],
        compiler_params=params,
        cost_estimate=cost,
        name="tables_last",
    )(*blocks, before)


def finish_kernel(parts_ref, out_ref):
    summed = jnp.sum(parts_ref[...], axis=0)
    row = lax.broadcasted_iota(jnp.int32, (128, 256), 0)
    col = lax.broadcasted_iota(jnp.int32, (128, 256), 1)
    same_half = (row >= COLS) == (col >= 128)
    lane = jnp.where(row >= COLS, row - COLS, row)
    target = jnp.where(col >= 128, col - 128, col)
    even = (target % 2) == 0
    inside = same_half & (target < 96)
    entry = jnp.where(inside & (target // 2 == lane), jnp.where(even, -1.0, 1.0), 0.0)
    entry = entry + jnp.where(inside & even & (lane == 48), 2.0, 0.0)
    spread = jnp.dot(
        summed, entry, precision=lax.Precision.HIGHEST, preferred_element_type=jnp.float32
    )
    third_row = spread[72:96, :96]
    singles = spread[72:80, 128:224]
    ones_row = singles[0:1]

    def gain(total):
        return 1.0 - total / (3.0 * F)

    gain_partner = gain(ones_row) * (4.5 / (8.0 * F))
    third_total = summed[72:96, 48:49]
    own_total = summed[72:80, 112:113]
    third_gain = (gain(2.0 * F - third_total), gain(third_total))
    own_gain = (gain(2.0 * F - own_total), gain(own_total))
    for i in range(SHARE):
        half, ii = divmod(i, 3)
        pair = spread[ii * VB : (ii + 1) * VB, half * 128 : half * 128 + 96]
        own_row = singles[1 + i : 2 + i]
        by_place = {
            (1, 1): pair,
            (1, 0): 2.0 * own_row - pair,
            (0, 1): 2.0 * third_row - pair,
            (0, 0): (4.0 * ones_row - 2.0 * own_row) - (2.0 * third_row - pair),
        }
        for a in range(2):
            partner = gain_partner * own_gain[a][1 + i : 2 + i]
            for c in range(2):
                out_ref[i, a, pl.ds(c, VB, stride=2), :] = by_place[a, c] * third_gain[c] * partner


def finish(parts):
    return pl.pallas_call(
        finish_kernel,
        out_shape=jax.ShapeDtypeStruct((SHARE, 2, 2 * VB, 96), jnp.float32),
        name="finish",
    )(parts)


def body(dosage):
    rep_plane = lax.axis_index("rep")
    width = dosage.shape[1] // N_REP // CHUNKS
    own = [
        lax.dynamic_slice_in_dim(dosage, (rep_plane * CHUNKS + n) * width, width, 1)
        for n in range(CHUNKS)
    ]
    near = [(shifted(u, 1), shifted(u, -1)) for u in own]
    far = [(shifted(a, 1), shifted(b, -1)) for a, b in near]
    state = None
    for u, (a1, b1), (a2, b2) in zip(own, near, far):
        state = tables_of((u, a1, a2, b1, b2), state)
    parts = lax.all_to_all(state, ("rep", "field"), split_axis=0, concat_axis=0, tiled=True)
    return finish(parts).reshape(1, SHARE, 2, VB, 2, 96)


def solution(mesh):
    return jax.shard_map(
        body,
        mesh=mesh,
        in_specs=(P("vec", "field"),),
        out_specs=P("rep", ("vec", "field"), None, None, None, None),
        check_vma=False,
    )
```

```python
import jax
import jax.numpy as jnp
from jax import lax
from jax.experimental import pallas as pl
from jax.experimental.pallas import tpu as pltpu
from jax.sharding import Mesh, PartitionSpec as P

F = 65536
VB = 24
N_VEC = 32
SHARE = 6
WIDTHS = (4096, 4096)
STEP = 1024
PAIRS = VB * 2 * VB
ROWS = PAIRS + 96
COLS = 64
PACKED = 96
SWAP = ((0, 1), (1, 0))


def swapped(value, odd):
    pairs = [(i, (((i + odd) ^ 1) - odd) % N_VEC) for i in range(N_VEC)]
    return lax.ppermute(value, "vec", pairs)


def to_chip(value, flip):
    return lax.ppermute(value, ("xlo", "rep"), [(i, i ^ flip) for i in range(4)])


def accumulate(u_ref, third_refs, partner_refs, lhs_ref, acc_ref, start):
    width = u_ref.shape[1]
    for at in range(0, width, STEP):
        step = min(STEP, width - at)
        cut = slice(at, at + step)
        own = u_ref[:, cut]
        third = jnp.concatenate([ref[:, cut] for ref in third_refs], axis=0)
        for i in range(VB):
            lhs_ref[i * 48 : (i + 1) * 48, :step] = own[i : i + 1, :] * third
        ones = jnp.ones((VB, step), jnp.bfloat16)
        lhs_ref[PAIRS:, :step] = jnp.concatenate([third, own, ones], axis=0)
        partner = jnp.concatenate([ref[:, cut] for ref in partner_refs] + [ones[:16]], axis=0)
        product = lax.dot_general(
            lhs_ref[:, :step], partner, (((1,), (1,)), ((), ())), preferred_element_type=jnp.float32
        )
        if at > 0:
            acc_ref[...] += product
        elif start is None:
            acc_ref[...] = product
        else:
            acc_ref[...] = start[...] + product


def pack(acc_ref, out_ref):
    for core in range(2):
        for chip in range(4):
            xlo, rep = divmod(chip, 2)
            q = xlo * 2 + core
            for ii in range(3):
                for half in range(2):
                    row = (SHARE * q + 3 * half + ii) * 48 + VB * rep
                    out_ref[core, chip, ii * VB : (ii + 1) * VB, half * COLS : (half + 1) * COLS] = (
                        acc_ref[row : row + VB, :]
                    )
            out_ref[core, chip, 72:96, :COLS] = acc_ref[PAIRS + VB * rep : PAIRS + VB * (rep + 1), :]
            out_ref[core, chip, 72:80, COLS:] = jnp.concatenate(
                [
                    acc_ref[PAIRS + 72 : PAIRS + 73, :],
                    acc_ref[PAIRS + 48 + SHARE * q : PAIRS + 48 + SHARE * (q + 1), :],
                    jnp.zeros((1, COLS), jnp.float32),
                ],
                axis=0,
            )
            out_ref[core, chip, 80:96, COLS:] = jnp.zeros((16, COLS), jnp.float32)


def tables_kernel(u_ref, a1_ref, a2_ref, b1_ref, b2_ref, *rest, first, last):
    start = None if first else rest[0]
    out_ref, lhs_ref = rest[-3 if last else -2], rest[-2 if last else -1]
    acc_ref = rest[-1] if last else out_ref
    accumulate(u_ref, (a1_ref, a2_ref), (b1_ref, b2_ref), lhs_ref, acc_ref, start)
    if last:
        pack(acc_ref, out_ref)


def tables_of(blocks, before, last):
    width = blocks[0].shape[1]
    first = before is None
    shape = (2, 4, PACKED, 128) if last else (ROWS, COLS)
    scratch = [pltpu.VMEM((ROWS, STEP), jnp.bfloat16)]
    if last:
        scratch.append(pltpu.VMEM((ROWS, COLS), jnp.float32))

    def kernel(*refs):
        tables_kernel(*refs, first=first, last=last)

    return pl.pallas_call(
        kernel,
        out_shape=jax.ShapeDtypeStruct(shape, jnp.float32),
        scratch_shapes=scratch,
        compiler_params=pltpu.CompilerParams(vmem_limit_bytes=32 * 2**20),
        cost_estimate=pl.CostEstimate(
            flops=2 * ROWS * width * 256, bytes_accessed=5 * VB * width * 2, transcendentals=0
        ),
        name="tables",
    )(*blocks, *(() if first else (before,)))


def finish_kernel(own_ref, one_ref, two_ref, three_ref, out_ref):
    summed = (own_ref[0] + one_ref[...]) + (two_ref[...] + three_ref[...])
    row = lax.broadcasted_iota(jnp.int32, (128, 256), 0)
    col = lax.broadcasted_iota(jnp.int32, (128, 256), 1)
    same_half = (row >= COLS) == (col >= 128)
    lane = jnp.where(row >= COLS, row - COLS, row)
    target = jnp.where(col >= 128, col - 128, col)
    even = (target % 2) == 0
    inside = same_half & (target < 96)
    entry = jnp.where(inside & (target // 2 == lane), jnp.where(even, -1.0, 1.0), 0.0)
    entry = entry + jnp.where(inside & even & (lane == 48), 2.0, 0.0)
    spread = jnp.dot(
        summed, entry, precision=lax.Precision.HIGHEST, preferred_element_type=jnp.float32
    )
    third_row = spread[72:96, :96]
    singles = spread[72:80, 128:224]
    ones_row = singles[0:1]

    def gain(total):
        return 1.0 - total / (3.0 * F)

    gain_partner = gain(ones_row) * (4.5 / (8.0 * F))
    third_total = summed[72:96, 48:49]
    own_total = summed[72:80, 112:113]
    third_gain = (gain(2.0 * F - third_total), gain(third_total))
    own_gain = (gain(2.0 * F - own_total), gain(own_total))
    for i in range(SHARE):
        half, ii = divmod(i, 3)
        pair = spread[ii * VB : (ii + 1) * VB, half * 128 : half * 128 + 96]
        own_row = singles[1 + i : 2 + i]
        by_place = {
            (1, 1): pair,
            (1, 0): 2.0 * own_row - pair,
            (0, 1): 2.0 * third_row - pair,
            (0, 0): (4.0 * ones_row - 2.0 * own_row) - (2.0 * third_row - pair),
        }
        for a in range(2):
            partner = gain_partner * own_gain[a][1 + i : 2 + i]
            for c in range(2):
                out_ref[i, a, pl.ds(c, VB, stride=2), :] = by_place[a, c] * third_gain[c] * partner


def finish(parts):
    return pl.pallas_call(
        finish_kernel,
        out_shape=jax.ShapeDtypeStruct((SHARE, 2, 2 * VB, 96), jnp.float32),
        name="finish",
    )(*parts)


def body(dosage):
    rep = lax.axis_index("rep")
    core = lax.axis_index("core")
    chip = lax.axis_index("xlo") * 2 + rep
    even = lax.axis_index("vec") % 2 == 0
    half = dosage.shape[1] // 2
    own, at = [], 0
    for width in WIDTHS:
        own.append(lax.dynamic_slice_in_dim(dosage, rep * half + at, width, 1))
        at += width
    near = [(swapped(u, 0), swapped(u, 1)) for u in own]
    far = [(swapped(o, 0), swapped(e, 1)) for e, o in near]
    near = [(jnp.where(even, o, e), jnp.where(even, e, o)) for e, o in near]
    far = [(jnp.where(even, o, e), jnp.where(even, e, o)) for e, o in far]
    state = None
    for n, (u, (a1, b1), (a2, b2)) in enumerate(zip(own, near, far)):
        state = tables_of((u, a1, a2, b1, b2), state, n == len(WIDTHS) - 1)
    kept = lax.dynamic_index_in_dim(state, core, 0, False)
    sent = lax.dynamic_index_in_dim(state, 1 - core, 0, False)
    kept = kept + lax.ppermute(sent, "core", SWAP)
    parts = [lax.dynamic_slice_in_dim(kept, chip, 1, 0)]
    for flip in (1, 3, 2):
        parts.append(to_chip(lax.dynamic_index_in_dim(kept, chip ^ flip, 0, False), flip))
    return finish(parts).reshape(1, SHARE, 2, VB, 2, 96)


def solution(mesh):
    split = Mesh(mesh.devices.reshape(N_VEC, 2, 2, 2), ("vec", "xlo", "core", "rep"))
    return jax.shard_map(
        body,
        mesh=split,
        in_specs=(P("vec", ("xlo", "core")),),
        out_specs=P("rep", ("vec", "xlo", "core"), None, None, None, None),
        check_vma=False,
    )
```

```python
import jax
import jax.numpy as jnp
from jax import lax
from jax.experimental import pallas as pl
from jax.experimental.pallas import tpu as pltpu
from jax.sharding import Mesh, PartitionSpec as P

F = 65536
VB = 24
N_VEC = 32
SHARE = 6
WIDTHS = (4096, 4096)
STEP = 1024
PAIRS = VB * 2 * VB
ROWS = PAIRS + 96
COLS = 64
PACKED = 96
SWAP = ((0, 1), (1, 0))


def swapped(value, odd):
    pairs = [(i, (((i + odd) ^ 1) - odd) % N_VEC) for i in range(N_VEC)]
    return lax.ppermute(value, "vec", pairs)


def to_chip(value, flip):
    return lax.ppermute(value, ("xlo", "rep"), [(i, i ^ flip) for i in range(4)])


def accumulate(u_ref, third_refs, partner_refs, lhs_ref, acc_ref, start):
    width = u_ref.shape[1]
    for at in range(0, width, STEP):
        step = min(STEP, width - at)
        cut = slice(at, at + step)
        own = u_ref[:, cut]
        third = jnp.concatenate([ref[:, cut] for ref in third_refs], axis=0)
        for i in range(VB):
            lhs_ref[i * 48 : (i + 1) * 48, :step] = own[i : i + 1, :] * third
        ones = jnp.ones((VB, step), jnp.bfloat16)
        lhs_ref[PAIRS:, :step] = jnp.concatenate([third, own, ones], axis=0)
        partner = jnp.concatenate([ref[:, cut] for ref in partner_refs] + [ones[:16]], axis=0)
        product = lax.dot_general(
            lhs_ref[:, :step], partner, (((1,), (1,)), ((), ())), preferred_element_type=jnp.float32
        )
        if at > 0:
            acc_ref[...] += product
        elif start is None:
            acc_ref[...] = product
        else:
            acc_ref[...] = start[...] + product


def pack(acc_ref, out_ref):
    for core in range(2):
        for chip in range(4):
            xlo, rep = divmod(chip, 2)
            q = xlo * 2 + core
            for ii in range(3):
                for half in range(2):
                    row = (SHARE * q + 3 * half + ii) * 48 + VB * rep
                    out_ref[core, chip, ii * VB : (ii + 1) * VB, half * COLS : (half + 1) * COLS] = (
                        acc_ref[row : row + VB, :]
                    )
            out_ref[core, chip, 72:96, :COLS] = acc_ref[PAIRS + VB * rep : PAIRS + VB * (rep + 1), :]
            out_ref[core, chip, 72:80, COLS:] = jnp.concatenate(
                [
                    acc_ref[PAIRS + 72 : PAIRS + 73, :],
                    acc_ref[PAIRS + 48 + SHARE * q : PAIRS + 48 + SHARE * (q + 1), :],
                    jnp.zeros((1, COLS), jnp.float32),
                ],
                axis=0,
            )
            out_ref[core, chip, 80:96, COLS:] = jnp.zeros((16, COLS), jnp.float32)


def tables_kernel(u_ref, a1_ref, a2_ref, b1_ref, b2_ref, *rest, first, last):
    start = None if first else rest[0]
    out_ref, lhs_ref = rest[-3 if last else -2], rest[-2 if last else -1]
    acc_ref = rest[-1] if last else out_ref
    accumulate(u_ref, (a1_ref, a2_ref), (b1_ref, b2_ref), lhs_ref, acc_ref, start)
    if last:
        pack(acc_ref, out_ref)


def tables_of(blocks, before, last):
    width = blocks[0].shape[1]
    first = before is None
    shape = (2, 4, PACKED, 128) if last else (ROWS, COLS)
    scratch = [pltpu.VMEM((ROWS, STEP), jnp.bfloat16)]
    if last:
        scratch.append(pltpu.VMEM((ROWS, COLS), jnp.float32))

    def kernel(*refs):
        tables_kernel(*refs, first=first, last=last)

    return pl.pallas_call(
        kernel,
        out_shape=jax.ShapeDtypeStruct(shape, jnp.float32),
        scratch_shapes=scratch,
        compiler_params=pltpu.CompilerParams(vmem_limit_bytes=32 * 2**20),
        cost_estimate=pl.CostEstimate(
            flops=2 * ROWS * width * 256, bytes_accessed=5 * VB * width * 2, transcendentals=0
        ),
        name="tables",
    )(*blocks, *(() if first else (before,)))


def finish_kernel(own_ref, one_ref, two_ref, three_ref, out_ref):
    summed = (own_ref[0] + one_ref[...]) + (two_ref[...] + three_ref[...])
    row = lax.broadcasted_iota(jnp.int32, (128, 256), 0)
    col = lax.broadcasted_iota(jnp.int32, (128, 256), 1)
    same_half = (row >= COLS) == (col >= 128)
    lane = jnp.where(row >= COLS, row - COLS, row)
    target = jnp.where(col >= 128, col - 128, col)
    even = (target % 2) == 0
    inside = same_half & (target < 96)
    entry = jnp.where(inside & (target // 2 == lane), jnp.where(even, -1.0, 1.0), 0.0)
    entry = entry + jnp.where(inside & even & (lane == 48), 2.0, 0.0)
    spread = jnp.dot(
        summed, entry, precision=lax.Precision.HIGHEST, preferred_element_type=jnp.float32
    )
    third_row = spread[72:96, :96]
    singles = spread[72:80, 128:224]
    ones_row = singles[0:1]

    def gain(total):
        return 1.0 - total / (3.0 * F)

    gain_partner = gain(ones_row) * (4.5 / (8.0 * F))
    third_total = summed[72:96, 48:49]
    own_total = summed[72:80, 112:113]
    third_gain = (gain(2.0 * F - third_total), gain(third_total))
    own_gain = (gain(2.0 * F - own_total), gain(own_total))
    for i in range(SHARE):
        half, ii = divmod(i, 3)
        pair = spread[ii * VB : (ii + 1) * VB, half * 128 : half * 128 + 96]
        own_row = singles[1 + i : 2 + i]
        by_place = {
            (1, 1): pair,
            (1, 0): 2.0 * own_row - pair,
            (0, 1): 2.0 * third_row - pair,
            (0, 0): (4.0 * ones_row - 2.0 * own_row) - (2.0 * third_row - pair),
        }
        for a in range(2):
            partner = gain_partner * own_gain[a][1 + i : 2 + i]
            for c in range(2):
                out_ref[i, a, pl.ds(c, VB, stride=2), :] = by_place[a, c] * third_gain[c] * partner


def finish(parts):
    return pl.pallas_call(
        finish_kernel,
        out_shape=jax.ShapeDtypeStruct((SHARE, 2, 2 * VB, 96), jnp.float32),
        compiler_params=pltpu.CompilerParams(vmem_limit_bytes=8 * 2**20),
        name="finish",
    )(*parts)


def body(dosage):
    rep = lax.axis_index("rep")
    core = lax.axis_index("core")
    chip = lax.axis_index("xlo") * 2 + rep
    even = lax.axis_index("vec") % 2 == 0
    half = dosage.shape[1] // 2
    own, at = [], 0
    for width in WIDTHS:
        own.append(lax.dynamic_slice_in_dim(dosage, rep * half + at, width, 1))
        dosage, own[-1] = lax.optimization_barrier((dosage, own[-1]))
        at += width
    near = [(swapped(u, 0), swapped(u, 1)) for u in own]
    far = [(swapped(o, 0), swapped(e, 1)) for e, o in near]
    near = [(jnp.where(even, o, e), jnp.where(even, e, o)) for e, o in near]
    far = [(jnp.where(even, o, e), jnp.where(even, e, o)) for e, o in far]
    state = None
    for n, (u, (a1, b1), (a2, b2)) in enumerate(zip(own, near, far)):
        state = tables_of((u, a1, a2, b1, b2), state, n == len(WIDTHS) - 1)
    kept = lax.dynamic_index_in_dim(state, core, 0, False)
    sent = lax.dynamic_index_in_dim(state, 1 - core, 0, False)
    kept = kept + lax.ppermute(sent, "core", SWAP)
    parts = [lax.dynamic_slice_in_dim(kept, chip, 1, 0)]
    for flip in (2, 3, 1):
        parts.append(to_chip(lax.dynamic_index_in_dim(kept, chip ^ flip, 0, False), flip))
    return finish(parts).reshape(1, SHARE, 2, VB, 2, 96)


def solution(mesh):
    split = Mesh(mesh.devices.reshape(N_VEC, 2, 2, 2), ("vec", "xlo", "core", "rep"))
    return jax.shard_map(
        body,
        mesh=split,
        in_specs=(P("vec", ("xlo", "core")),),
        out_specs=P("rep", ("vec", "xlo", "core"), None, None, None, None),
        check_vma=False,
    )
```

```python
import jax
import jax.numpy as jnp
from jax import lax
from jax.experimental import pallas as pl
from jax.experimental.pallas import tpu as pltpu
from jax.sharding import Mesh, PartitionSpec as P

F = 65536
VB = 24
N_VEC = 32
SHARE = 6
E_WIDTHS = (4096, 4096)
O_WIDTHS = (4096, 4096)
SPANS = (4096, 4096)
STEP = 256
STREAMED = 9
CUT = STREAMED * 48 + 48
HELD = (VB - STREAMED) * 48 + 32
OWN = CUT + (VB - STREAMED) * 48
ROWS = CUT + HELD
COLS = 64
PACKED = 96
SWAP = ((0, 1), (1, 0))


def swapped(value, odd):
    pairs = [(i, (((i + odd) ^ 1) - odd) % N_VEC) for i in range(N_VEC)]
    return lax.ppermute(value, "vec", pairs)


def to_chip(value, flip):
    return lax.ppermute(value, ("xlo", "rep"), [(i, i ^ flip) for i in range(4)])


def taken(pieces, at, step):
    for start, ref in pieces:
        if start <= at < start + ref.shape[1]:
            return ref[:, at - start : at - start + step]


def accumulate(streams, span, acc_ref, held_ref, before):
    even = lax.axis_index("vec") % 2 == 0
    for at in range(*span, STEP):
        own, e, o, oe, eo = (taken(pieces, at, STEP) for pieces in streams)
        third = jnp.concatenate([jnp.where(even, o, e), jnp.where(even, oe, eo)], axis=0)
        ones = jnp.ones((16, STEP), jnp.bfloat16)
        partner = jnp.concatenate(
            [jnp.where(even, e, o), jnp.where(even, eo, oe), ones], axis=0
        )
        pairs = [own[i : i + 1, :] * third for i in range(VB)]
        streamed = jnp.concatenate(pairs[:STREAMED] + [third], axis=0)
        held = jnp.concatenate(pairs[STREAMED:] + [own, ones[:8]], axis=0)
        first = lax.dot_general(
            streamed, partner, (((1,), (1,)), ((), ())), preferred_element_type=jnp.float32
        )
        second = lax.dot_general(
            partner, held, (((1,), (1,)), ((), ())), preferred_element_type=jnp.float32
        )
        if at > span[0]:
            acc_ref[:CUT, :] += first
            held_ref[...] += second
        elif before is None:
            acc_ref[:CUT, :] = first
            held_ref[...] = second
        else:
            acc_ref[:CUT, :] = before[0][:CUT, :] + first
            held_ref[...] = before[1][...] + second


def row_of(i):
    return i * 48 if i < STREAMED else CUT + (i - STREAMED) * 48


def pack(acc_ref, out_ref):
    for core in range(2):
        for chip in range(4):
            xlo, rep = divmod(chip, 2)
            q = xlo * 2 + core
            for ii in range(3):
                for half in range(2):
                    row = row_of(SHARE * q + 3 * half + ii) + VB * rep
                    out_ref[core, chip, ii * VB : (ii + 1) * VB, half * COLS : (half + 1) * COLS] = (
                        acc_ref[row : row + VB, :]
                    )
            out_ref[core, chip, 72:96, :COLS] = acc_ref[STREAMED * 48 + VB * rep : STREAMED * 48 + VB * (rep + 1), :]
            out_ref[core, chip, 72:80, COLS:] = jnp.concatenate(
                [
                    acc_ref[OWN + VB : OWN + VB + 1, :],
                    acc_ref[OWN + SHARE * q : OWN + SHARE * (q + 1), :],
                    jnp.zeros((1, COLS), jnp.float32),
                ],
                axis=0,
            )
            out_ref[core, chip, 80:96, COLS:] = jnp.zeros((16, COLS), jnp.float32)


def tables_of(streams, span, before, last):
    picked = [
        [(start, piece) for start, piece in stream if start < span[1] and start + piece.shape[1] > span[0]]
        for stream in streams
    ]
    order = (0, 1, 2, 3, 4)
    blocks = [piece for k in order for _, piece in picked[k]]

    def kernel(*refs):
        refs = list(refs)
        found = [None] * len(picked)
        for k in order:
            found[k] = [(start, refs.pop(0)) for start, _ in picked[k]]
        before_refs = None if before is None else (refs.pop(0), refs.pop(0))
        if last:
            out_ref, acc_ref, held_ref = refs
        else:
            acc_ref, held_ref = refs
        accumulate(found, span, acc_ref, held_ref, before_refs)
        if last:
            acc_ref[CUT:, :] = held_ref[...].T
            pack(acc_ref, out_ref)

    sums = [(CUT if not last else ROWS, COLS), (COLS, HELD)]
    packed = jax.ShapeDtypeStruct((2, 4, PACKED, 128), jnp.float32)
    width = span[1] - span[0]
    return pl.pallas_call(
        kernel,
        out_shape=packed if last else [jax.ShapeDtypeStruct(shape, jnp.float32) for shape in sums],
        scratch_shapes=[pltpu.VMEM(shape, jnp.float32) for shape in sums] if last else [],
        compiler_params=pltpu.CompilerParams(vmem_limit_bytes=32 * 2**20),
        cost_estimate=pl.CostEstimate(
            flops=2 * ROWS * width * 256, bytes_accessed=5 * VB * width * 2, transcendentals=0
        ),
        name="tables",
    )(*blocks, *(() if before is None else before))


def finish_kernel(own_ref, one_ref, two_ref, three_ref, out_ref):
    summed = (own_ref[0] + one_ref[...]) + (two_ref[...] + three_ref[...])
    row = lax.broadcasted_iota(jnp.int32, (128, 256), 0)
    col = lax.broadcasted_iota(jnp.int32, (128, 256), 1)
    same_half = (row >= COLS) == (col >= 128)
    lane = jnp.where(row >= COLS, row - COLS, row)
    target = jnp.where(col >= 128, col - 128, col)
    even = (target % 2) == 0
    inside = same_half & (target < 96)
    entry = jnp.where(inside & (target // 2 == lane), jnp.where(even, -1.0, 1.0), 0.0)
    entry = entry + jnp.where(inside & even & (lane == 48), 2.0, 0.0)
    spread = jnp.dot(
        summed, entry, precision=lax.Precision.HIGHEST, preferred_element_type=jnp.float32
    )
    third_row = spread[72:96, :96]
    singles = spread[72:80, 128:224]
    ones_row = singles[0:1]

    def gain(total):
        return 1.0 - total / (3.0 * F)

    gain_partner = gain(ones_row) * (4.5 / (8.0 * F))
    third_total = summed[72:96, 48:49]
    own_total = summed[72:80, 112:113]
    third_gain = (gain(2.0 * F - third_total), gain(third_total))
    own_gain = (gain(2.0 * F - own_total), gain(own_total))
    for i in range(SHARE):
        half, ii = divmod(i, 3)
        pair = spread[ii * VB : (ii + 1) * VB, half * 128 : half * 128 + 96]
        own_row = singles[1 + i : 2 + i]
        by_place = {
            (1, 1): pair,
            (1, 0): 2.0 * own_row - pair,
            (0, 1): 2.0 * third_row - pair,
            (0, 0): (4.0 * ones_row - 2.0 * own_row) - (2.0 * third_row - pair),
        }
        for a in range(2):
            partner = gain_partner * own_gain[a][1 + i : 2 + i]
            for c in range(2):
                out_ref[i, a, pl.ds(c, VB, stride=2), :] = by_place[a, c] * third_gain[c] * partner


def finish(parts):
    return pl.pallas_call(
        finish_kernel,
        out_shape=jax.ShapeDtypeStruct((SHARE, 2, 2 * VB, 96), jnp.float32),
        compiler_params=pltpu.CompilerParams(vmem_limit_bytes=8 * 2**20),
        name="finish",
    )(*parts)


def body(dosage):
    rep = lax.axis_index("rep")
    core = lax.axis_index("core")
    chip = lax.axis_index("xlo") * 2 + rep
    half = dosage.shape[1] // 2

    def cut(dosage, at, width):
        piece = lax.dynamic_slice_in_dim(dosage, rep * half + at, width, 1)
        return lax.optimization_barrier((dosage, piece))

    def pieces(widths):
        at = 0
        for width in widths:
            yield at, width
            at += width

    own = []
    for at, width in pieces(E_WIDTHS):
        dosage, piece = cut(dosage, at, width)
        own.append((at, piece))
    e_own = o_own = own

    e = [(at, swapped(u, 0)) for at, u in e_own]
    o = [(at, swapped(u, 1)) for at, u in o_own]
    eo = [(at, swapped(v, 0)) for at, v in o]
    oe = [(at, swapped(v, 1)) for at, v in e]
    state = None
    for at, width in pieces(SPANS):
        span = (at, at + width)
        state = tables_of((e_own, e, o, oe, eo), span, state, span[1] == half)
    kept = lax.dynamic_index_in_dim(state, core, 0, False)
    sent = lax.dynamic_index_in_dim(state, 1 - core, 0, False)
    kept = kept + lax.ppermute(sent, "core", SWAP)
    parts = [lax.dynamic_slice_in_dim(kept, chip, 1, 0)]
    for flip in (2, 3, 1):
        parts.append(to_chip(lax.dynamic_index_in_dim(kept, chip ^ flip, 0, False), flip))
    return finish(parts).reshape(1, SHARE, 2, VB, 2, 96)


def solution(mesh):
    split = Mesh(mesh.devices.reshape(N_VEC, 2, 2, 2), ("vec", "xlo", "core", "rep"))
    return jax.shard_map(
        body,
        mesh=split,
        in_specs=(P("vec", ("xlo", "core")),),
        out_specs=P("rep", ("vec", "xlo", "core"), None, None, None, None),
        check_vma=False,
    )
```

```python
import jax
import jax.numpy as jnp
from jax import lax
from jax.experimental import pallas as pl
from jax.experimental.pallas import tpu as pltpu
from jax.sharding import Mesh, PartitionSpec as P

F = 65536
VB = 24
N_VEC = 32
SHARE = 6
E_WIDTHS = (4096, 4096)
O_WIDTHS = (4096, 4096)
SPANS = (4096, 4096)
STEP = 256
STREAMED = 9
CUT = STREAMED * 48 + 48
HELD = (VB - STREAMED) * 48 + 32
OWN = CUT + (VB - STREAMED) * 48
ROWS = CUT + HELD
COLS = 64
PACKED = 96
SWAP = ((0, 1), (1, 0))


def swapped(value, odd):
    pairs = [(i, (((i + odd) ^ 1) - odd) % N_VEC) for i in range(N_VEC)]
    return lax.ppermute(value, "vec", pairs)


def to_chip(value, flip):
    return lax.ppermute(value, ("xlo", "rep"), [(i, i ^ flip) for i in range(4)])


def taken(pieces, at, step):
    for start, ref in pieces:
        if start <= at < start + ref.shape[1]:
            return ref[:, at - start : at - start + step]


def accumulate(streams, span, acc_ref, held_ref, before):
    even = lax.axis_index("vec") % 2 == 0
    for at in range(*span, STEP):
        own, e, o, oe, eo = (taken(pieces, at, STEP) for pieces in streams)
        third = jnp.concatenate([jnp.where(even, o, e), jnp.where(even, oe, eo)], axis=0)
        ones = jnp.ones((16, STEP), jnp.bfloat16)
        partner = jnp.concatenate(
            [jnp.where(even, e, o), jnp.where(even, eo, oe), ones], axis=0
        )
        pairs = [own[i : i + 1, :] * third for i in range(VB)]
        streamed = jnp.concatenate(pairs[:STREAMED] + [third], axis=0)
        held = jnp.concatenate(pairs[STREAMED:] + [own, ones[:8]], axis=0)
        first = lax.dot_general(
            streamed, partner, (((1,), (1,)), ((), ())), preferred_element_type=jnp.float32
        )
        second = lax.dot_general(
            partner, held, (((1,), (1,)), ((), ())), preferred_element_type=jnp.float32
        )
        if at > span[0]:
            acc_ref[:CUT, :] += first
            held_ref[...] += second
        elif before is None:
            acc_ref[:CUT, :] = first
            held_ref[...] = second
        else:
            acc_ref[:CUT, :] = before[0][:CUT, :] + first
            held_ref[...] = before[1][...] + second


def rows(acc_ref, turned, at, count):
    if at < CUT:
        return acc_ref[at : at + count, :]
    return turned[at - CUT : at - CUT + count]


def pack(acc_ref, turned, out_ref):
    for core in range(2):
        for chip in range(4):
            xlo, rep = divmod(chip, 2)
            q = xlo * 2 + core
            for ii in range(3):
                for half in range(2):
                    i = SHARE * q + 3 * half + ii
                    row = i * 48 + VB * rep + (48 if i >= STREAMED else 0)
                    out_ref[core, chip, ii * VB : (ii + 1) * VB, half * COLS : (half + 1) * COLS] = (
                        rows(acc_ref, turned, row, VB)
                    )
            out_ref[core, chip, 72:96, :COLS] = acc_ref[STREAMED * 48 + VB * rep : STREAMED * 48 + VB * (rep + 1), :]
            out_ref[core, chip, 72:80, COLS:] = jnp.concatenate(
                [
                    rows(acc_ref, turned, OWN + VB, 1),
                    rows(acc_ref, turned, OWN + SHARE * q, SHARE),
                    jnp.zeros((1, COLS), jnp.float32),
                ],
                axis=0,
            )
            out_ref[core, chip, 80:96, COLS:] = jnp.zeros((16, COLS), jnp.float32)


def tables_of(streams, span, before, last):
    picked = [
        [(start, piece) for start, piece in stream if start < span[1] and start + piece.shape[1] > span[0]]
        for stream in streams
    ]
    order = (0, 1, 2, 3, 4)
    blocks = [piece for k in order for _, piece in picked[k]]

    def kernel(*refs):
        refs = list(refs)
        found = [None] * len(picked)
        for k in order:
            found[k] = [(start, refs.pop(0)) for start, _ in picked[k]]
        before_refs = None if before is None else (refs.pop(0), refs.pop(0))
        if last:
            out_ref, acc_ref, held_ref = refs
        else:
            acc_ref, held_ref = refs
        accumulate(found, span, acc_ref, held_ref, before_refs)
        if last:
            pack(acc_ref, held_ref[...].T, out_ref)

    sums = [(CUT, COLS), (COLS, HELD)]
    packed = jax.ShapeDtypeStruct((2, 4, PACKED, 128), jnp.float32)
    width = span[1] - span[0]
    return pl.pallas_call(
        kernel,
        out_shape=packed if last else [jax.ShapeDtypeStruct(shape, jnp.float32) for shape in sums],
        scratch_shapes=[pltpu.VMEM(shape, jnp.float32) for shape in sums] if last else [],
        compiler_params=pltpu.CompilerParams(vmem_limit_bytes=32 * 2**20),
        cost_estimate=pl.CostEstimate(
            flops=2 * ROWS * width * 256, bytes_accessed=5 * VB * width * 2, transcendentals=0
        ),
        name="tables",
    )(*blocks, *(() if before is None else before))


def finish_kernel(own_ref, one_ref, two_ref, three_ref, out_ref):
    summed = (own_ref[0] + one_ref[...]) + (two_ref[...] + three_ref[...])
    row = lax.broadcasted_iota(jnp.int32, (128, 256), 0)
    col = lax.broadcasted_iota(jnp.int32, (128, 256), 1)
    same_half = (row >= COLS) == (col >= 128)
    lane = jnp.where(row >= COLS, row - COLS, row)
    target = jnp.where(col >= 128, col - 128, col)
    even = (target % 2) == 0
    inside = same_half & (target < 96)
    entry = jnp.where(inside & (target // 2 == lane), jnp.where(even, -1.0, 1.0), 0.0)
    entry = entry + jnp.where(inside & even & (lane == 48), 2.0, 0.0)
    high = summed.astype(jnp.bfloat16)
    rest = summed - high.astype(jnp.float32)
    middle = rest.astype(jnp.bfloat16)
    low = (rest - middle.astype(jnp.float32)).astype(jnp.bfloat16)
    products = jnp.dot(
        jnp.concatenate([high, middle, low], axis=0),
        entry.astype(jnp.bfloat16),
        preferred_element_type=jnp.float32,
    )
    spread = products[:PACKED] + (products[PACKED : 2 * PACKED] + products[2 * PACKED :])
    third_row = spread[72:96, :96]
    singles = spread[72:80, 128:224]
    ones_row = singles[0:1]

    def gain(total):
        return 1.0 - total / (3.0 * F)

    gain_partner = gain(ones_row) * (4.5 / (8.0 * F))
    third_total = summed[72:96, 48:49]
    own_total = summed[72:80, 112:113]
    third_gain = (gain(2.0 * F - third_total), gain(third_total))
    own_gain = (gain(2.0 * F - own_total), gain(own_total))
    for i in range(SHARE):
        half, ii = divmod(i, 3)
        pair = spread[ii * VB : (ii + 1) * VB, half * 128 : half * 128 + 96]
        own_row = singles[1 + i : 2 + i]
        by_place = {
            (1, 1): pair,
            (1, 0): 2.0 * own_row - pair,
            (0, 1): 2.0 * third_row - pair,
            (0, 0): (4.0 * ones_row - 2.0 * own_row) - (2.0 * third_row - pair),
        }
        for a in range(2):
            partner = gain_partner * own_gain[a][1 + i : 2 + i]
            for c in range(2):
                out_ref[i, a, pl.ds(c, VB, stride=2), :] = by_place[a, c] * third_gain[c] * partner


def finish(parts):
    return pl.pallas_call(
        finish_kernel,
        out_shape=jax.ShapeDtypeStruct((SHARE, 2, 2 * VB, 96), jnp.float32),
        compiler_params=pltpu.CompilerParams(vmem_limit_bytes=8 * 2**20),
        name="finish",
    )(*parts)


def body(dosage):
    rep = lax.axis_index("rep")
    core = lax.axis_index("core")
    chip = lax.axis_index("xlo") * 2 + rep
    half = dosage.shape[1] // 2

    def cut(dosage, at, width):
        piece = lax.dynamic_slice_in_dim(dosage, rep * half + at, width, 1)
        return lax.optimization_barrier((dosage, piece))

    def pieces(widths):
        at = 0
        for width in widths:
            yield at, width
            at += width

    own = []
    for at, width in pieces(E_WIDTHS):
        dosage, piece = cut(dosage, at, width)
        own.append((at, piece))
    e_own = o_own = own

    e = [(at, swapped(u, 0)) for at, u in e_own]
    o = [(at, swapped(u, 1)) for at, u in o_own]
    eo = [(at, swapped(v, 0)) for at, v in o]
    oe = [(at, swapped(v, 1)) for at, v in e]
    state = None
    for at, width in pieces(SPANS):
        span = (at, at + width)
        state = tables_of((e_own, e, o, oe, eo), span, state, span[1] == half)
    kept = lax.dynamic_index_in_dim(state, core, 0, False)
    sent = lax.dynamic_index_in_dim(state, 1 - core, 0, False)
    kept = kept + lax.ppermute(sent, "core", SWAP)
    parts = [lax.dynamic_slice_in_dim(kept, chip, 1, 0)]
    for flip in (2, 3, 1):
        parts.append(to_chip(lax.dynamic_index_in_dim(kept, chip ^ flip, 0, False), flip))
    return finish(parts).reshape(1, SHARE, 2, VB, 2, 96)


def solution(mesh):
    split = Mesh(mesh.devices.reshape(N_VEC, 2, 2, 2), ("vec", "xlo", "core", "rep"))
    return jax.shard_map(
        body,
        mesh=split,
        in_specs=(P("vec", ("xlo", "core")),),
        out_specs=P("rep", ("vec", "xlo", "core"), None, None, None, None),
        check_vma=False,
    )
```
